32 devices in a mesh: grp: 2 (over y), blk: 4 (over z), head: 4 (over x, core).
Axes of the slice: x: 2, y: 2, z: 4, core: 2. Of those that a mesh axis runs over, the one named last changes fastest.
Arguments:
- queries: bfloat16 [256, 16384], P(('grp', 'blk'), 'head'), parts along dimension 0, may hold values from -80 to 80
- kv_cache: bfloat16 [64, 512, 8, 256], P(('grp', 'blk'), None, 'head'), parts along dimension 0, may hold values from -4 to 4
- draft_kv: bfloat16 [64, 4, 8, 256], P(('grp', 'blk'), None, 'head'), parts along dimension 0, may hold values from -5 to 5
- cache_len: int32 [64], P(('grp', 'blk')), parts along dimension 0, may hold values from 2 to 512, as said below
- accepted: int32 [64, 4], P(('grp', 'blk')), parts along dimension 0, may hold values from 0 to 1, as said below
- w_out: bfloat16 [16384, 16384], P('head', 'blk'), may hold values from -0.046875 to 0.046875
- residual: bfloat16 [256, 16384], P(('grp', 'head'), 'blk'), parts along dimension 0, may hold values from -12 to 12
- norm_gain: bfloat16 [16384], P('blk'), may hold values from 0.5 to 1.5
Outputs:
- residual_out: bfloat16 [256, 16384], P(('grp', 'head'), 'blk'), parts along dimension 0
- normed: bfloat16 [256, 16384], P(('grp', 'head'), 'blk'), parts along dimension 0
The draws below stay inside these ranges and needn't reach their ends.
There are 2 independent parts, one for each index of `grp`. The reference program is written for one: setup_inputs(seed, part) draws one part's arguments, and reference() takes and returns one part's arrays. A program takes and returns all parts, laid end to end along the dimension named above; an argument that names none is the same for every part. Nothing has to cross between parts.
Inputs may be any that keep to these rules, and one draw needn't show every extreme that they name: `cache_len`: every sequence has at least two live slots; in every draw some sequences of every index of blk use all 512 slots. `accepted`: each row holds ones followed by zeros.
All inputs are finite; a program needn't handle non-finite values.
Results may differ from the reference program's by a relative error of at most 0.0038.
Values may be sent and summed in bfloat16 or wider, within the bound.
A program may use at most 128 MiB of HBM per device.

```python
import jax
import jax.numpy as jnp
from jax import lax

D = 16384
HQ = 128
KVH = 8
HD = 128
DRAFT = 4
CTX = 512
SEQS = 32
ROWS = 128


def cache_key_table(key):
    return jnp.clip(jax.random.normal(key, (SEQS, CTX, KVH, HD), jnp.float32), -4.0, 4.0)


def draw_kv_cache(key, part):
    key_table = cache_key_table(key)
    key = jax.random.fold_in(key, 11)
    value_table = jnp.clip(jax.random.normal(key, (SEQS, CTX, KVH, HD), jnp.float32), -4.0, 4.0)
    return jnp.concatenate([key_table, value_table], axis=-1).astype(jnp.bfloat16)


def draw_queries(key, part):
    key = jax.random.fold_in(key, 12)
    result = jnp.clip(3.0 * jax.random.normal(key, (ROWS, HQ * HD), jnp.float32), -12.0, 12.0)
    return result.astype(jnp.bfloat16)


def draw_cache_len(key, part):
    key = jax.random.fold_in(key, 13)
    drawn = jax.random.randint(key, (SEQS,), 2, CTX + 1, dtype=jnp.int32)
    full_rows = jnp.arange(SEQS) % 3 == 0
    return jnp.where(full_rows, CTX, drawn).astype(jnp.int32)


def draw_accepted(key, part):
    key = jax.random.fold_in(key, 14)
    prefix = jax.random.randint(key, (SEQS, 1), 0, DRAFT + 1, dtype=jnp.int32)
    return (jnp.arange(DRAFT, dtype=jnp.int32)[None, :] < prefix).astype(jnp.int32)


def draw_residual(key, part):
    key = jax.random.fold_in(key, 15)
    column_key = jax.random.fold_in(key, 1)
    entry_key = jax.random.fold_in(key, 3)
    spread = jax.random.uniform(column_key, (D,), jnp.float32, 0.0, 1.0)
    trend = jnp.arange(D, dtype=jnp.float32) / D
    column_scale = 0.1 * jnp.power(10.0, spread) * jnp.power(3.0, trend)
    entries = jnp.clip(jax.random.normal(entry_key, (ROWS, D), jnp.float32), -4.0, 4.0)
    return (entries * column_scale[None, :]).astype(jnp.bfloat16)


def steps_of(own_key, extent, cuts, least, largest):
    def one(position, shards_of):
        heights = jax.random.uniform(jax.random.fold_in(jax.random.fold_in(own_key, 6), position), (shards_of,), jnp.float32, least / len(cuts), largest / len(cuts))
        return jnp.repeat(jnp.exp(heights), extent[position] // shards_of).reshape((-1,) + (1,) * (len(extent) - position - 1))

    loudness = one(*cuts[0])
    for cut in cuts[1:]:
        loudness = loudness * one(*cut)
    return loudness


def centred(key, dims, scale, reach, shards=(), kind=jnp.bfloat16):
    values = scale * jax.random.normal(key, dims, jnp.float32)
    if shards:
        values = values * steps_of(key, dims, shards, -0.22, 0.18)
    return jnp.clip(values, -reach, reach).astype(kind)


def setup_inputs(seed: int = 0, part: int = 0) -> dict:
    key_of = jax.random.split(jax.random.key(seed), 9)
    part_keys = jax.random.split(jax.random.fold_in(key_of[8], part), 9)
    return {
        "queries": draw_queries(jax.random.fold_in(jax.random.fold_in(key_of[8], part), 71), part),
        "kv_cache": draw_kv_cache(jax.random.fold_in(jax.random.fold_in(key_of[8], part), 71), part),
        "draft_kv": centred(part_keys[2], (SEQS, DRAFT, KVH, 2 * HD), 1.0, 5.0, ((0, 4), (2, 4))),
        "cache_len": draw_cache_len(jax.random.fold_in(jax.random.fold_in(key_of[8], part), 71), part),
        "accepted": draw_accepted(jax.random.fold_in(jax.random.fold_in(key_of[8], part), 71), part),
        "w_out": centred(key_of[5], (HQ * HD, D), (HQ * HD) ** -0.5, 0.046875, ((0, 4), (1, 4))),
        "residual": draw_residual(jax.random.fold_in(jax.random.fold_in(key_of[8], part), 71), part),
        "norm_gain": jnp.clip(1.0 + 0.1 * jax.random.normal(key_of[7], (D,), jnp.float32), 0.5, 1.5).astype(jnp.bfloat16),
    }


def attend(query_rows, cache_rows, draft_rows, length, accept_row):
    head_dim = cache_rows.shape[-1] // 2
    scaling = head_dim ** (-0.5)
    query_f = query_rows.astype(jnp.float32)
    cache_keys = cache_rows[..., :head_dim].astype(jnp.float32)
    cache_values = cache_rows[..., head_dim:].astype(jnp.float32)
    draft_keys = draft_rows[..., :head_dim].astype(jnp.float32)
    draft_values = draft_rows[..., head_dim:].astype(jnp.float32)
    cache_scores = jnp.einsum('jkgd,pkd->kjgp', query_f, cache_keys) * scaling
    draft_scores = jnp.einsum('jkgd,ikd->kjgi', query_f, draft_keys) * scaling
    slots = jnp.arange(cache_rows.shape[0], dtype=jnp.int32)
    cache_scores = jnp.where(slots < length, cache_scores, -1e+30)
    draft_len = draft_rows.shape[0]
    later = jnp.arange(draft_len, dtype=jnp.int32)[:, None]
    earlier = jnp.arange(draft_len, dtype=jnp.int32)[None, :]
    visible = (earlier == later) | (earlier < later) & (accept_row[None, :] == 1)
    draft_scores = jnp.where(visible[None, :, None, :], draft_scores, -1e+30)
    top_score = jnp.maximum(lax.optimization_barrier(jnp.max(cache_scores, axis=-1)), lax.optimization_barrier(jnp.max(draft_scores, axis=-1)))[..., None]
    cache_exp = jnp.exp(cache_scores - top_score)
    draft_exp = jnp.exp(draft_scores - top_score)
    totals = lax.optimization_barrier(jnp.sum(cache_exp, axis=-1, keepdims=True)) + lax.optimization_barrier(jnp.sum(draft_exp, axis=-1, keepdims=True))
    cache_probs = (cache_exp / totals).astype(jnp.bfloat16).astype(jnp.float32)
    draft_probs = (draft_exp / totals).astype(jnp.bfloat16).astype(jnp.float32)
    context = jnp.einsum('kjgp,pkd->jkgd', cache_probs, cache_values)
    context = context + jnp.einsum('kjgi,ikd->jkgd', draft_probs, draft_values)
    return context.astype(jnp.bfloat16).reshape(draft_len, -1)

def reference(queries, kv_cache, draft_kv, cache_len, accepted, w_out, residual, norm_gain):
    query_rows = queries.reshape(SEQS, DRAFT, KVH, HQ // KVH, HD)

    def one_sequence(bundle):
        return attend(bundle[0], bundle[1], bundle[2], bundle[3], bundle[4])
    context = lax.map(one_sequence, (query_rows, kv_cache, draft_kv, cache_len, accepted))
    context = context.reshape(ROWS, HQ * HD)
    attended = jnp.dot(context, w_out, preferred_element_type=jnp.float32)
    summed = residual.astype(jnp.float32) + attended
    mean_square = lax.optimization_barrier(jnp.mean(summed * summed, axis=1, keepdims=True))
    normed = summed * lax.rsqrt(mean_square + 1e-05) * norm_gain.astype(jnp.float32)
    return (summed.astype(jnp.bfloat16), normed.astype(jnp.bfloat16))
```

```python
import functools

import jax
import jax.numpy as jnp
from jax import lax
from jax.experimental import pallas as pl
from jax.experimental.pallas import tpu as pltpu
from jax.sharding import PartitionSpec as P

MESH = pl.DeviceIdType.MESH
CHUNKS = 4
TILE = 512


def attend_local(query_rows, cache_rows, draft_rows, length, accept_row):
    head_dim = cache_rows.shape[-1] // 2
    scaling = head_dim ** (-0.5)
    cache_keys = cache_rows[..., :head_dim]
    cache_values = cache_rows[..., head_dim:]
    draft_keys = draft_rows[..., :head_dim]
    draft_values = draft_rows[..., head_dim:]
    cache_scores = (
        jnp.einsum("jkgd,pkd->kjgp", query_rows, cache_keys, preferred_element_type=jnp.float32)
        * scaling
    )
    draft_scores = (
        jnp.einsum("jkgd,ikd->kjgi", query_rows, draft_keys, preferred_element_type=jnp.float32)
        * scaling
    )
    slots = jnp.arange(cache_rows.shape[0], dtype=jnp.int32)
    cache_scores = jnp.where(slots < length, cache_scores, -1e30)
    draft_len = draft_rows.shape[0]
    later = jnp.arange(draft_len, dtype=jnp.int32)[:, None]
    earlier = jnp.arange(draft_len, dtype=jnp.int32)[None, :]
    visible = (earlier == later) | (earlier < later) & (accept_row[None, :] == 1)
    draft_scores = jnp.where(visible[None, :, None, :], draft_scores, -1e30)
    top_score = jnp.maximum(jnp.max(cache_scores, axis=-1), jnp.max(draft_scores, axis=-1))[
        ..., None
    ]
    cache_exp = jnp.exp(cache_scores - top_score)
    draft_exp = jnp.exp(draft_scores - top_score)
    totals = jnp.sum(cache_exp, axis=-1, keepdims=True) + jnp.sum(draft_exp, axis=-1, keepdims=True)
    cache_probs = (cache_exp / totals).astype(jnp.bfloat16)
    draft_probs = (draft_exp / totals).astype(jnp.bfloat16)
    context = jnp.einsum(
        "kjgp,pkd->jkgd", cache_probs, cache_values, preferred_element_type=jnp.float32
    )
    context = context + jnp.einsum(
        "kjgi,ikd->jkgd", draft_probs, draft_values, preferred_element_type=jnp.float32
    )
    return context.astype(jnp.bfloat16).reshape(draft_len, -1)


def project_kernel(
    blocks, heads,
    ctx_ref, w_ref, res_ref, gain_ref, out_ref, norm_ref,
    gat, wv, acc, send_a, recv_a, send_b, recv_b, squares,
    w_sem, up_s, up_r, dn_s, dn_r, a_s, a_r, b_s, b_r, q_s, q_r,
):
    rows, depth = ctx_ref.shape
    wide = w_ref.shape[1]
    own_rows = res_ref.shape[0]
    kc = depth // CHUNKS
    nt = min(TILE, wide)
    tiles = wide // nt
    pairs = heads // 2
    blk = lax.axis_index("blk")
    head = lax.axis_index("head")
    side = lax.rem(head, 2)
    chip = head // 2
    partner = chip * 2 + (1 - side)
    full = wide * blocks

    def w_copy(c):
        part = pl.ds(c * kc, kc)
        return pltpu.make_async_copy(w_ref.at[part], wv.at[part], w_sem.at[c])

    def up_copy(t, c, src=None):
        block = lax.rem(blk - t + blocks, blocks)
        cols = pl.ds(pl.multiple_of(c * kc, kc), kc)
        src = gat.at[block, :, cols] if src is None else src.at[:, cols]
        n = t * CHUNKS + c
        return pltpu.make_async_remote_copy(
            src, gat.at[block, :, cols], up_s.at[n], up_r.at[n],
            device_id={"blk": lax.rem(blk + 1, blocks)}, device_id_type=MESH)

    def dn_copy(t, c, src=None):
        block = lax.rem(blk + t, blocks)
        cols = pl.ds(pl.multiple_of(c * kc, kc), kc)
        src = gat.at[block, :, cols] if src is None else src.at[:, cols]
        n = t * CHUNKS + c
        return pltpu.make_async_remote_copy(
            src, gat.at[block, :, cols], dn_s.at[n], dn_r.at[n],
            device_id={"blk": lax.rem(blk + blocks - 1, blocks)}, device_id_type=MESH)

    def up_wait(t, c):
        block = lax.rem(blk - 1 - t + blocks, blocks)
        cols = pl.ds(pl.multiple_of(c * kc, kc), kc)
        n = t * CHUNKS + c
        pltpu.make_async_remote_copy(
            gat.at[block, :, cols], gat.at[block, :, cols], up_s.at[n], up_r.at[n],
            device_id={"blk": lax.rem(blk + 1, blocks)}, device_id_type=MESH).wait_recv()

    def dn_wait(t, c):
        block = lax.rem(blk + 1 + t, blocks)
        cols = pl.ds(pl.multiple_of(c * kc, kc), kc)
        n = t * CHUNKS + c
        pltpu.make_async_remote_copy(
            gat.at[block, :, cols], gat.at[block, :, cols], dn_s.at[n], dn_r.at[n],
            device_id={"blk": lax.rem(blk + 1, blocks)}, device_id_type=MESH).wait_recv()

    for c in range(CHUNKS):
        w_copy(c).start()

    barrier = pltpu.get_barrier_semaphore()
    for k in range(1, blocks):
        pl.semaphore_signal(barrier, inc=1, device_id={"blk": lax.rem(blk + k, blocks)},
                            device_id_type=MESH)
    pl.semaphore_signal(barrier, inc=1, device_id={"head": partner}, device_id_type=MESH)
    for k in range(1, pairs):
        pl.semaphore_signal(
            barrier, inc=1,
            device_id={"head": lax.rem(chip + k, pairs) * 2 + side}, device_id_type=MESH)
    pl.semaphore_wait(barrier, blocks - 1 + 1 + pairs - 1)

    for c in range(CHUNKS):
        @pl.when(blk + 1 < blocks)
        def _():
            up_copy(0, c, ctx_ref).start()

        @pl.when(blk > 0)
        def _():
            dn_copy(0, c, ctx_ref).start()

    gat[pl.ds(blk, 1)] = ctx_ref[...][None]

    inner = jnp.logical_and(blk > 0, blk + 1 < blocks)

    def forward(n, carry):
        t = n // CHUNKS
        c = lax.rem(n, CHUNKS)

        @pl.when(jnp.logical_and(inner, blk - 1 - t >= 0))
        def _():
            up_wait(t, c)
            up_copy(t + 1, c).start()

        @pl.when(jnp.logical_and(inner, blk + 1 + t < blocks))
        def _():
            dn_wait(t, c)
            dn_copy(t + 1, c).start()

        return carry

    lax.fori_loop(0, (blocks - 2) * CHUNKS, forward, 0)

    def arrived(c):
        w_copy(c).wait()

        def one(t, carry):
            @pl.when(blk == blocks - 1)
            def _():
                up_wait(t, c)

            @pl.when(blk == 0)
            def _():
                dn_wait(t, c)

            return carry

        lax.fori_loop(0, blocks - 1, one, 0)

    def product(c, n):
        x = gat[:, :, c * kc:(c + 1) * kc].reshape(blocks * rows, kc)
        return jnp.dot(x, wv[c * kc:(c + 1) * kc, n], preferred_element_type=jnp.float32)

    for c in range(CHUNKS - 1):
        arrived(c)

        def tile_of(j, carry):
            n = pl.ds(pl.multiple_of(j * nt, nt), nt)
            if c == 0:
                acc[:, n] = product(c, n)
            else:
                acc[:, n] = acc[:, n] + product(c, n)
            return carry

        lax.fori_loop(0, tiles, tile_of, 0)

    arrived(CHUNKS - 1)

    def a_copy(j):
        return pltpu.make_async_remote_copy(
            send_a.at[j], recv_a.at[j], a_s.at[j], a_r.at[j],
            device_id={"head": partner}, device_id_type=MESH)

    def b_copy(j, k):
        to = lax.rem(chip + k, pairs)
        n = j * (pairs - 1) + k - 1
        return pltpu.make_async_remote_copy(
            send_b.at[n], recv_b.at[n], b_s.at[n], b_r.at[n],
            device_id={"head": to * 2 + side}, device_id_type=MESH)

    def pair_sum(j):
        n = pl.ds(pl.multiple_of(j * nt, nt), nt)
        a_copy(j).wait_recv()
        for k in range(pairs):
            to = lax.rem(chip + k, pairs)
            at = pl.ds(pl.multiple_of((to * 2 + side) * own_rows, own_rows), own_rows)
            total = acc[at, n] + recv_a[j, to].astype(jnp.float32)
            if k == 0:
                acc[at, n] = total
            else:
                send_b[j * (pairs - 1) + k - 1] = total.astype(jnp.bfloat16)
                b_copy(j, k).start()

    def last(j, carry):
        n = pl.ds(pl.multiple_of(j * nt, nt), nt)
        acc[:, n] = acc[:, n] + product(CHUNKS - 1, n)
        for x in range(pairs):
            at = pl.ds(pl.multiple_of((x * 2 + 1 - side) * own_rows, own_rows), own_rows)
            send_a[j, x] = acc[at, n].astype(jnp.bfloat16)
        a_copy(j).start()

        @pl.when(j > 0)
        def _():
            pair_sum(j - 1)

        return carry

    lax.fori_loop(0, tiles, last, 0)
    pair_sum(tiles - 1)

    squares[blk] = jnp.zeros((own_rows, 128), jnp.float32)
    mine = pl.ds(pl.multiple_of(head * own_rows, own_rows), own_rows)

    def finish(j, carry):
        n = pl.ds(pl.multiple_of(j * nt, nt), nt)
        total = acc[mine, n]
        for k in range(1, pairs):
            b_copy(j, k).wait_recv()
            total = total + recv_b[j * (pairs - 1) + k - 1].astype(jnp.float32)
        total = total + res_ref[:, n].astype(jnp.float32)
        acc[mine, n] = total
        out_ref[:, n] = total.astype(jnp.bfloat16)
        power = total * total
        part = power[:, 0:128]
        for v in range(1, nt // 128):
            part = part + power[:, v * 128:(v + 1) * 128]
        squares[blk] = squares[blk] + part
        return carry

    lax.fori_loop(0, tiles, finish, 0)

    def q_copy(k):
        return pltpu.make_async_remote_copy(
            squares.at[blk], squares.at[blk], q_s.at[k - 1], q_r.at[k - 1],
            device_id={"blk": lax.rem(blk + k, blocks)}, device_id_type=MESH)

    for k in range(1, blocks):
        q_copy(k).start()
    for k in range(1, blocks):
        src = lax.rem(blk - k + blocks, blocks)
        pltpu.make_async_remote_copy(
            squares.at[src], squares.at[src], q_s.at[k - 1], q_r.at[k - 1],
            device_id={"blk": lax.rem(blk + k, blocks)}, device_id_type=MESH).wait_recv()

    spread = squares[0]
    for b in range(1, blocks):
        spread = spread + squares[b]
    inverse = lax.rsqrt(jnp.sum(spread, axis=1, keepdims=True) / full + 1e-5)

    def scale(j, carry):
        n = pl.ds(pl.multiple_of(j * nt, nt), nt)
        norm_ref[:, n] = (acc[mine, n] * inverse * gain_ref[:, n].astype(jnp.float32)).astype(
            jnp.bfloat16)
        return carry

    lax.fori_loop(0, tiles, scale, 0)

    for c in range(CHUNKS):
        @pl.when(blk + 1 < blocks)
        def _():
            up_copy(0, c, ctx_ref).wait_send()

        @pl.when(blk > 0)
        def _():
            dn_copy(0, c, ctx_ref).wait_send()

    def forwarded(n, carry):
        t = n // CHUNKS
        c = lax.rem(n, CHUNKS)

        @pl.when(jnp.logical_and(inner, blk - 1 - t >= 0))
        def _():
            up_copy(t + 1, c).wait_send()

        @pl.when(jnp.logical_and(inner, blk + 1 + t < blocks))
        def _():
            dn_copy(t + 1, c).wait_send()

        return carry

    lax.fori_loop(0, (blocks - 2) * CHUNKS, forwarded, 0)

    def tile_sent(j, carry):
        a_copy(j).wait_send()
        for k in range(1, pairs):
            b_copy(j, k).wait_send()
        return carry

    lax.fori_loop(0, tiles, tile_sent, 0)
    for k in range(1, blocks):
        q_copy(k).wait_send()


def project(blocks, heads, context, w_out, residual, norm_gain):
    rows, depth = context.shape
    wide = w_out.shape[1]
    own_rows = residual.shape[0]
    nt = min(TILE, wide)
    tiles = wide // nt
    pairs = heads // 2
    hops = (blocks - 1) * CHUNKS
    cross = max(tiles * (pairs - 1), 1)
    dma = pltpu.SemaphoreType.DMA
    vmem = pl.BlockSpec(memory_space=pltpu.VMEM)
    shape = jax.ShapeDtypeStruct((own_rows, wide), jnp.bfloat16)
    return pl.pallas_call(
        functools.partial(project_kernel, blocks, heads),
        out_shape=(shape, shape),
        in_specs=[vmem, pl.BlockSpec(memory_space=pl.ANY), vmem, vmem],
        out_specs=(vmem, vmem),
        scratch_shapes=[
            pltpu.VMEM((blocks, rows, depth), jnp.bfloat16),
            pltpu.VMEM((depth, wide), jnp.bfloat16),
            pltpu.VMEM((blocks * rows, wide), jnp.float32),
            pltpu.VMEM((tiles, pairs, own_rows, nt), jnp.bfloat16),
            pltpu.VMEM((tiles, pairs, own_rows, nt), jnp.bfloat16),
            pltpu.VMEM((cross, own_rows, nt), jnp.bfloat16),
            pltpu.VMEM((cross, own_rows, nt), jnp.bfloat16),
            pltpu.VMEM((blocks, own_rows, 128), jnp.float32),
            dma((CHUNKS,)),
            dma((hops,)), dma((hops,)), dma((hops,)), dma((hops,)),
            dma((tiles,)), dma((tiles,)),
            dma((cross,)), dma((cross,)),
            dma((blocks - 1,)), dma((blocks - 1,)),
        ],
        compiler_params=pltpu.CompilerParams(
            collective_id=0, has_side_effects=True, vmem_limit_bytes=56 * 2**20),
        cost_estimate=pl.CostEstimate(
            flops=2 * blocks * rows * depth * wide, bytes_accessed=2 * depth * wide,
            transcendentals=0),
        name="project",
    )(context, w_out, residual, norm_gain.reshape(1, wide))


def local(blocks, heads, queries, kv_cache, draft_kv, cache_len, accepted, w_out, residual,
          norm_gain):
    seq_count = kv_cache.shape[0]
    kv_local = kv_cache.shape[2]
    head_dim = kv_cache.shape[3] // 2
    draft_len = draft_kv.shape[1]
    group_size = queries.shape[1] // (kv_local * head_dim)
    query_rows = queries.reshape(seq_count, draft_len, kv_local, group_size, head_dim)
    context = jax.vmap(attend_local)(query_rows, kv_cache, draft_kv, cache_len, accepted)
    context = context.reshape(seq_count * draft_len, -1)
    return project(blocks, heads, context, w_out, residual, norm_gain)


def solution(mesh):
    return jax.shard_map(
        functools.partial(local, mesh.shape["blk"], mesh.shape["head"]),
        mesh=mesh,
        in_specs=(
            P(("grp", "blk"), "head"),
            P(("grp", "blk"), None, "head", None),
            P(("grp", "blk"), None, "head", None),
            P(("grp", "blk")),
            P(("grp", "blk"), None),
            P("head", "blk"),
            P(("grp", "head"), "blk"),
            P("blk"),
        ),
        out_specs=(P(("grp", "head"), "blk"), P(("grp", "head"), "blk")),
        check_vma=False,
    )
```

```python
import functools

import jax
import jax.numpy as jnp
from jax import lax
from jax.experimental import pallas as pl
from jax.experimental.pallas import tpu as pltpu
from jax.sharding import PartitionSpec as P

MESH = pl.DeviceIdType.MESH
CHUNKS = 4
TILE = 1024


def attention(scr, q_ref, kv_ref, draft_ref, len_ref, acc_ref, gat, blk):
    keys, vals, qf, qs, cf, k_sem, v_sem = scr
    seqs, slots, kvh, two = kv_ref.shape
    hd = two // 2
    drafts = draft_ref.shape[1]
    heads = q_ref.shape[1] // hd
    group = heads // kvh
    n = group * drafts
    cols = slots * kvh
    scaling = hd ** (-0.5)
    over_last = (((1,), (1,)), ((), ()))

    def copies(s):
        return (
            pltpu.make_async_copy(kv_ref.at[s, :, :, pl.ds(0, hd)], keys.at[s], k_sem.at[s]),
            pltpu.make_async_copy(kv_ref.at[s, :, :, pl.ds(hd, hd)], vals.at[s], v_sem.at[s]),
        )

    def load():
        for s in range(seqs):
            for copy in copies(s):
                copy.start()

    def prepare():
        qf[...] = q_ref[...].astype(jnp.float32)
        for s in range(seqs):
            for h in range(heads):
                qs[s, h * drafts:(h + 1) * drafts, :] = (
                    qf[s * drafts:(s + 1) * drafts, h * hd:(h + 1) * hd])

    def one_head(kh):
        col = lax.broadcasted_iota(jnp.int32, (n, cols), 1)
        slot = jnp.where(col % kvh == kh, col // kvh, 2**30)
        shape = (n, drafts * kvh)
        j = lax.broadcasted_iota(jnp.int32, shape, 0) % drafts
        dcol = lax.broadcasted_iota(jnp.int32, shape, 1)
        i = dcol // kvh
        mine = dcol % kvh == kh
        for s in range(seqs):
            if kh == 0:
                for copy in copies(s):
                    copy.wait()
            q = qs[s, kh * n:(kh + 1) * n, :].astype(jnp.bfloat16)
            k = keys[s].reshape(cols, hd)
            v = vals[s].reshape(cols, hd)
            d = draft_ref[s].astype(jnp.float32).reshape(drafts * kvh, two).astype(jnp.bfloat16)
            scores = lax.dot_general(
                q, k, over_last, preferred_element_type=jnp.float32) * scaling
            scores = jnp.where(slot < len_ref[s], scores, -1e30)
            draft_scores = lax.dot_general(
                q, d[:, :hd], over_last, preferred_element_type=jnp.float32) * scaling
            taken = jnp.zeros(shape, jnp.int32)
            for x in range(drafts):
                taken = jnp.where(i == x, acc_ref[s, x], taken)
            visible = mine & ((i == j) | ((i < j) & (taken == 1)))
            draft_scores = jnp.where(visible, draft_scores, -1e30)
            top = jnp.maximum(jnp.max(scores, axis=1, keepdims=True),
                              jnp.max(draft_scores, axis=1, keepdims=True))
            e = jnp.exp(scores - top)
            de = jnp.exp(draft_scores - top)
            inverse = 1.0 / (jnp.sum(e, axis=1, keepdims=True)
                             + jnp.sum(de, axis=1, keepdims=True))
            out = jnp.dot((e * inverse).astype(jnp.bfloat16), v,
                          preferred_element_type=jnp.float32)
            out = out + jnp.dot((de * inverse).astype(jnp.bfloat16), d[:, hd:],
                                preferred_element_type=jnp.float32)
            for g in range(group):
                h = kh * group + g
                cf[s * drafts:(s + 1) * drafts, h * hd:(h + 1) * hd] = (
                    out[g * drafts:(g + 1) * drafts, :])
        at = slice(kh * group * hd, (kh + 1) * group * hd)
        gat[pl.ds(blk, 1), :, at] = cf[:, at].astype(jnp.bfloat16)[None]

    return load, prepare, one_head


def project_kernel(
    blocks, heads,
    q_ref, kv_ref, draft_ref, len_ref, acc_ref, w_ref, res_ref, sum_ref, inv_ref,
    keys, vals, qf, qs, cf, k_sem, v_sem,
    gat, wv, acc, send_a, recv_a, send_b, recv_b, squares,
    w_sem, up_s, up_r, dn_s, dn_r, a_s, a_r, b_s, b_r, q_s, q_r,
):
    rows, depth = q_ref.shape
    kvh = kv_ref.shape[2]
    ready = CHUNKS // kvh
    wide = w_ref.shape[1]
    own_rows = res_ref.shape[0]
    kc = depth // CHUNKS
    nt = min(TILE, wide)
    tiles = wide // nt
    pairs = heads // 2
    blk = lax.axis_index("blk")
    head = lax.axis_index("head")
    side = lax.rem(head, 2)
    chip = head // 2
    partner = chip * 2 + (1 - side)
    full = wide * blocks

    def w_copy(c):
        part = pl.ds(c * kc, kc)
        return pltpu.make_async_copy(w_ref.at[part], wv.at[part], w_sem.at[c])

    def up_copy(t, c):
        block = lax.rem(blk - t + blocks, blocks)
        cols = pl.ds(pl.multiple_of(c * kc, kc), kc)
        src = gat.at[block, :, cols]
        n = t * CHUNKS + c
        return pltpu.make_async_remote_copy(
            src, gat.at[block, :, cols], up_s.at[n], up_r.at[n],
            device_id={"blk": lax.rem(blk + 1, blocks)}, device_id_type=MESH)

    def dn_copy(t, c):
        block = lax.rem(blk + t, blocks)
        cols = pl.ds(pl.multiple_of(c * kc, kc), kc)
        src = gat.at[block, :, cols]
        n = t * CHUNKS + c
        return pltpu.make_async_remote_copy(
            src, gat.at[block, :, cols], dn_s.at[n], dn_r.at[n],
            device_id={"blk": lax.rem(blk + blocks - 1, blocks)}, device_id_type=MESH)

    def up_wait(t, c):
        block = lax.rem(blk - 1 - t + blocks, blocks)
        cols = pl.ds(pl.multiple_of(c * kc, kc), kc)
        n = t * CHUNKS + c
        pltpu.make_async_remote_copy(
            gat.at[block, :, cols], gat.at[block, :, cols], up_s.at[n], up_r.at[n],
            device_id={"blk": lax.rem(blk + 1, blocks)}, device_id_type=MESH).wait_recv()

    def dn_wait(t, c):
        block = lax.rem(blk + 1 + t, blocks)
        cols = pl.ds(pl.multiple_of(c * kc, kc), kc)
        n = t * CHUNKS + c
        pltpu.make_async_remote_copy(
            gat.at[block, :, cols], gat.at[block, :, cols], dn_s.at[n], dn_r.at[n],
            device_id={"blk": lax.rem(blk + 1, blocks)}, device_id_type=MESH).wait_recv()

    load, prepare, one_head = attention(
        (keys, vals, qf, qs, cf, k_sem, v_sem),
        q_ref, kv_ref, draft_ref, len_ref, acc_ref, gat, blk)
    load()
    for c in range(CHUNKS):
        w_copy(c).start()

    barrier = pltpu.get_barrier_semaphore()
    for k in range(1, blocks):
        pl.semaphore_signal(barrier, inc=1, device_id={"blk": lax.rem(blk + k, blocks)},
                            device_id_type=MESH)
    pl.semaphore_signal(barrier, inc=1, device_id={"head": partner}, device_id_type=MESH)
    for k in range(1, pairs):
        pl.semaphore_signal(
            barrier, inc=1,
            device_id={"head": lax.rem(chip + k, pairs) * 2 + side}, device_id_type=MESH)
    prepare()
    one_head(0)
    pl.semaphore_wait(barrier, blocks - 1 + 1 + pairs - 1)

    inner = jnp.logical_and(blk > 0, blk + 1 < blocks)

    def send_own(c):
        @pl.when(blk + 1 < blocks)
        def _():
            up_copy(0, c).start()

        @pl.when(blk > 0)
        def _():
            dn_copy(0, c).start()

    def forward(c):
        def one(t, carry):
            @pl.when(jnp.logical_and(inner, blk - 1 - t >= 0))
            def _():
                up_wait(t, c)
                up_copy(t + 1, c).start()

            @pl.when(jnp.logical_and(inner, blk + 1 + t < blocks))
            def _():
                dn_wait(t, c)
                dn_copy(t + 1, c).start()

            return carry

        lax.fori_loop(0, blocks - 2, one, 0)

    ahead = min(2, ready)
    for c in range(ahead):
        send_own(c)
    for kh in range(1, kvh):
        one_head(kh)

    def arrived(c):
        w_copy(c).wait()

        def one(t, carry):
            @pl.when(blk == blocks - 1)
            def _():
                up_wait(t, c)

            @pl.when(blk == 0)
            def _():
                dn_wait(t, c)

            return carry

        lax.fori_loop(0, blocks - 1, one, 0)

    def product(c, n):
        x = gat[:, :, c * kc:(c + 1) * kc].reshape(blocks * rows, kc)
        return jnp.dot(x, wv[c * kc:(c + 1) * kc, n], preferred_element_type=jnp.float32)

    def add_chunk(c):
        def tile_of(j, carry):
            n = pl.ds(pl.multiple_of(j * nt, nt), nt)
            if c == 0:
                acc[:, n] = product(c, n)
            else:
                acc[:, n] = acc[:, n] + product(c, n)
            return carry

        lax.fori_loop(0, tiles, tile_of, 0)

    for c in range(CHUNKS):
        forward(c)
        if c + ahead < CHUNKS:
            send_own(c + ahead)
        if c > 0:
            arrived(c - 1)
            add_chunk(c - 1)

    arrived(CHUNKS - 1)

    def a_copy(j):
        return pltpu.make_async_remote_copy(
            send_a.at[j], recv_a.at[j], a_s.at[j], a_r.at[j],
            device_id={"head": partner}, device_id_type=MESH)

    def b_copy(j, k):
        to = lax.rem(chip + k, pairs)
        n = j * (pairs - 1) + k - 1
        return pltpu.make_async_remote_copy(
            send_b.at[n], recv_b.at[n], b_s.at[n], b_r.at[n],
            device_id={"head": to * 2 + side}, device_id_type=MESH)

    def pair_sum(j):
        n = pl.ds(pl.multiple_of(j * nt, nt), nt)
        a_copy(j).wait_recv()
        for k in range(pairs):
            to = lax.rem(chip + k, pairs)
            at = pl.ds(pl.multiple_of((to * 2 + side) * own_rows, own_rows), own_rows)
            total = acc[at, n] + recv_a[j, to].astype(jnp.float32)
            if k == 0:
                acc[at, n] = total
            else:
                send_b[j * (pairs - 1) + k - 1] = total.astype(jnp.bfloat16)
                b_copy(j, k).start()

    def last(j, carry):
        n = pl.ds(pl.multiple_of(j * nt, nt), nt)
        acc[:, n] = acc[:, n] + product(CHUNKS - 1, n)
        for x in range(pairs):
            at = pl.ds(pl.multiple_of((x * 2 + 1 - side) * own_rows, own_rows), own_rows)
            send_a[j, x] = acc[at, n].astype(jnp.bfloat16)
        a_copy(j).start()

        @pl.when(j > 0)
        def _():
            pair_sum(j - 1)

        return carry

    lax.fori_loop(0, tiles, last, 0)
    pair_sum(tiles - 1)

    squares[blk] = jnp.zeros((own_rows, 128), jnp.float32)
    mine = pl.ds(pl.multiple_of(head * own_rows, own_rows), own_rows)

    def finish(j, carry):
        n = pl.ds(pl.multiple_of(j * nt, nt), nt)
        total = acc[mine, n]
        for k in range(1, pairs):
            b_copy(j, k).wait_recv()
            total = total + recv_b[j * (pairs - 1) + k - 1].astype(jnp.float32)
        total = total + res_ref[:, n].astype(jnp.float32)
        sum_ref[:, n] = total
        power = total * total
        part = power[:, 0:128]
        for v in range(1, nt // 128):
            part = part + power[:, v * 128:(v + 1) * 128]
        squares[blk] = squares[blk] + part
        return carry

    lax.fori_loop(0, tiles, finish, 0)

    def q_copy(k):
        return pltpu.make_async_remote_copy(
            squares.at[blk], squares.at[blk], q_s.at[k - 1], q_r.at[k - 1],
            device_id={"blk": lax.rem(blk + k, blocks)}, device_id_type=MESH)

    for k in range(1, blocks):
        q_copy(k).start()
    for k in range(1, blocks):
        src = lax.rem(blk - k + blocks, blocks)
        pltpu.make_async_remote_copy(
            squares.at[src], squares.at[src], q_s.at[k - 1], q_r.at[k - 1],
            device_id={"blk": lax.rem(blk + k, blocks)}, device_id_type=MESH).wait_recv()

    spread = squares[0]
    for b in range(1, blocks):
        spread = spread + squares[b]
    inverse = lax.rsqrt(jnp.sum(spread, axis=1, keepdims=True) / full + 1e-5)
    inv_ref[...] = jnp.broadcast_to(inverse, inv_ref.shape)

    for c in range(CHUNKS):
        @pl.when(blk + 1 < blocks)
        def _():
            up_copy(0, c).wait_send()

        @pl.when(blk > 0)
        def _():
            dn_copy(0, c).wait_send()

    def forwarded(n, carry):
        t = n // CHUNKS
        c = lax.rem(n, CHUNKS)

        @pl.when(jnp.logical_and(inner, blk - 1 - t >= 0))
        def _():
            up_copy(t + 1, c).wait_send()

        @pl.when(jnp.logical_and(inner, blk + 1 + t < blocks))
        def _():
            dn_copy(t + 1, c).wait_send()

        return carry

    lax.fori_loop(0, (blocks - 2) * CHUNKS, forwarded, 0)

    def tile_sent(j, carry):
        a_copy(j).wait_send()
        for k in range(1, pairs):
            b_copy(j, k).wait_send()
        return carry

    lax.fori_loop(0, tiles, tile_sent, 0)
    for k in range(1, blocks):
        q_copy(k).wait_send()


def local(blocks, heads, queries, kv_cache, draft_kv, cache_len, accepted, w_out, residual,
          norm_gain):
    rows, depth = queries.shape
    seqs, slots, kvh, two = kv_cache.shape
    hd = two // 2
    drafts = draft_kv.shape[1]
    wide = w_out.shape[1]
    own_rows = residual.shape[0]
    nt = min(TILE, wide)
    tiles = wide // nt
    pairs = heads // 2
    hops = (blocks - 1) * CHUNKS
    cross = max(tiles * (pairs - 1), 1)
    dma = pltpu.SemaphoreType.DMA
    vmem = pl.BlockSpec(memory_space=pltpu.VMEM)
    smem = pl.BlockSpec(memory_space=pltpu.SMEM)
    anywhere = pl.BlockSpec(memory_space=pl.ANY)
    summed, inverse = pl.pallas_call(
        functools.partial(project_kernel, blocks, heads),
        out_shape=(
            jax.ShapeDtypeStruct((own_rows, wide), jnp.float32),
            jax.ShapeDtypeStruct((own_rows, 128), jnp.float32),
        ),
        in_specs=[vmem, anywhere, vmem, smem, smem, anywhere, vmem],
        out_specs=(vmem, vmem),
        scratch_shapes=[
            pltpu.VMEM((seqs, slots, kvh, hd), jnp.bfloat16),
            pltpu.VMEM((seqs, slots, kvh, hd), jnp.bfloat16),
            pltpu.VMEM((rows, depth), jnp.float32),
            pltpu.VMEM((seqs, depth // hd * drafts, hd), jnp.float32),
            pltpu.VMEM((rows, depth), jnp.float32),
            dma((seqs,)), dma((seqs,)),
            pltpu.VMEM((blocks, rows, depth), jnp.bfloat16),
            pltpu.VMEM((depth, wide), jnp.bfloat16),
            pltpu.VMEM((blocks * rows, wide), jnp.float32),
            pltpu.VMEM((tiles, pairs, own_rows, nt), jnp.bfloat16),
            pltpu.VMEM((tiles, pairs, own_rows, nt), jnp.bfloat16),
            pltpu.VMEM((cross, own_rows, nt), jnp.bfloat16),
            pltpu.VMEM((cross, own_rows, nt), jnp.bfloat16),
            pltpu.VMEM((blocks, own_rows, 128), jnp.float32),
            dma((CHUNKS,)),
            dma((hops,)), dma((hops,)), dma((hops,)), dma((hops,)),
            dma((tiles,)), dma((tiles,)),
            dma((cross,)), dma((cross,)),
            dma((blocks - 1,)), dma((blocks - 1,)),
        ],
        compiler_params=pltpu.CompilerParams(
            collective_id=0, has_side_effects=True, vmem_limit_bytes=56 * 2**20),
        cost_estimate=pl.CostEstimate(
            flops=2 * blocks * rows * depth * wide, bytes_accessed=2 * depth * wide,
            transcendentals=0),
        name="project",
    )(queries, kv_cache, draft_kv, cache_len, accepted, w_out, residual)
    normed = summed * inverse[:, :1] * norm_gain.astype(jnp.float32)[None, :]
    return (summed.astype(jnp.bfloat16), normed.astype(jnp.bfloat16))


def solution(mesh):
    return jax.shard_map(
        functools.partial(local, mesh.shape["blk"], mesh.shape["head"]),
        mesh=mesh,
        in_specs=(
            P(("grp", "blk"), "head"),
            P(("grp", "blk"), None, "head", None),
            P(("grp", "blk"), None, "head", None),
            P(("grp", "blk")),
            P(("grp", "blk"), None),
            P("head", "blk"),
            P(("grp", "head"), "blk"),
            P("blk"),
        ),
        out_specs=(P(("grp", "head"), "blk"), P(("grp", "head"), "blk")),
        check_vma=False,
    )
```

```python
import functools

import jax
import jax.numpy as jnp
from jax import lax
from jax.experimental import pallas as pl
from jax.experimental.pallas import tpu as pltpu
from jax.sharding import PartitionSpec as P

MESH = pl.DeviceIdType.MESH
CHUNKS = 2
TILE = 1024


def attention(scr, q_ref, kv_ref, draft_ref, len_ref, acc_ref, gat, blk):
    cache, qf, qs, cf, kv_sem = scr
    seqs, slots, kvh, two = kv_ref.shape
    hd = two // 2
    drafts = draft_ref.shape[1]
    heads = q_ref.shape[1] // hd
    group = heads // kvh
    n = group * drafts
    cols = slots * kvh
    scaling = hd ** (-0.5)
    over_last = (((1,), (1,)), ((), ()))

    def copies(s):
        return pltpu.make_async_copy(kv_ref.at[s], cache.at[s], kv_sem.at[s])

    def load():
        for s in range(seqs):
            copies(s).start()

    def prepare():
        qf[...] = q_ref[...].astype(jnp.float32)
        for s in range(seqs):
            for h in range(heads):
                qs[s, h * drafts:(h + 1) * drafts, :] = (
                    qf[s * drafts:(s + 1) * drafts, h * hd:(h + 1) * hd])

    def one_head(kh):
        col = lax.broadcasted_iota(jnp.int32, (n, cols), 1)
        slot = jnp.where(col % kvh == kh, col // kvh, 2**30)
        shape = (n, drafts * kvh)
        j = lax.broadcasted_iota(jnp.int32, shape, 0) % drafts
        dcol = lax.broadcasted_iota(jnp.int32, shape, 1)
        i = dcol // kvh
        mine = dcol % kvh == kh
        for s in range(seqs):
            if kh == 0:
                copies(s).wait()
            q = qs[s, kh * n:(kh + 1) * n, :].astype(jnp.bfloat16)
            k = cache[s, :, :, :hd].reshape(cols, hd)
            v = cache[s, :, :, hd:].reshape(cols, hd)
            d = draft_ref[s].astype(jnp.float32).reshape(drafts * kvh, two).astype(jnp.bfloat16)
            scores = lax.dot_general(
                q, k, over_last, preferred_element_type=jnp.float32) * scaling
            scores = jnp.where(slot < len_ref[s], scores, -1e30)
            draft_scores = lax.dot_general(
                q, d[:, :hd], over_last, preferred_element_type=jnp.float32) * scaling
            taken = jnp.zeros(shape, jnp.int32)
            for x in range(drafts):
                taken = jnp.where(i == x, acc_ref[x, s], taken)
            visible = mine & ((i == j) | ((i < j) & (taken == 1)))
            draft_scores = jnp.where(visible, draft_scores, -1e30)
            top = jnp.maximum(jnp.max(scores, axis=1, keepdims=True),
                              jnp.max(draft_scores, axis=1, keepdims=True))
            e = jnp.exp(scores - top)
            de = jnp.exp(draft_scores - top)
            inverse = 1.0 / (jnp.sum(e, axis=1, keepdims=True)
                             + jnp.sum(de, axis=1, keepdims=True))
            out = jnp.dot((e * inverse).astype(jnp.bfloat16), v,
                          preferred_element_type=jnp.float32)
            out = out + jnp.dot((de * inverse).astype(jnp.bfloat16), d[:, hd:],
                                preferred_element_type=jnp.float32)
            for g in range(group):
                h = kh * group + g
                cf[s * drafts:(s + 1) * drafts, h * hd:(h + 1) * hd] = (
                    out[g * drafts:(g + 1) * drafts, :])
        at = slice(kh * group * hd, (kh + 1) * group * hd)
        gat[pl.ds(blk, 1), :, at] = cf[:, at].astype(jnp.bfloat16)[None]

    return load, prepare, one_head


def project_kernel(
    blocks, heads,
    q_ref, kv_ref, draft_ref, len_ref, acc_ref, w_ref, res_ref, sum_ref, inv_ref,
    cache, qf, qs, cf, kv_sem,
    gat, wv, acc, send_a, recv_a, send_b, recv_b, squares,
    w_sem, up_s, up_r, dn_s, dn_r, a_s, a_r, b_s, b_r, q_s, q_r,
):
    rows, depth = q_ref.shape
    kvh = kv_ref.shape[2]
    ready = CHUNKS // kvh
    wide = w_ref.shape[1]
    own_rows = res_ref.shape[0]
    kc = depth // CHUNKS
    nt = min(TILE, wide)
    tiles = wide // nt
    pairs = heads // 2
    blk = lax.axis_index("blk")
    head = lax.axis_index("head")
    side = lax.rem(head, 2)
    chip = head // 2
    partner = chip * 2 + (1 - side)
    full = wide * blocks

    def w_copy(c):
        part = pl.ds(c * kc, kc)
        return pltpu.make_async_copy(w_ref.at[part], wv.at[part], w_sem.at[c])

    def up_copy(t, c):
        block = lax.rem(blk - t + blocks, blocks)
        cols = pl.ds(pl.multiple_of(c * kc, kc), kc)
        src = gat.at[block, :, cols]
        n = t * CHUNKS + c
        return pltpu.make_async_remote_copy(
            src, gat.at[block, :, cols], up_s.at[n], up_r.at[n],
            device_id={"blk": lax.rem(blk + 1, blocks)}, device_id_type=MESH)

    def dn_copy(t, c):
        block = lax.rem(blk + t, blocks)
        cols = pl.ds(pl.multiple_of(c * kc, kc), kc)
        src = gat.at[block, :, cols]
        n = t * CHUNKS + c
        return pltpu.make_async_remote_copy(
            src, gat.at[block, :, cols], dn_s.at[n], dn_r.at[n],
            device_id={"blk": lax.rem(blk + blocks - 1, blocks)}, device_id_type=MESH)

    def up_wait(t, c):
        block = lax.rem(blk - 1 - t + blocks, blocks)
        cols = pl.ds(pl.multiple_of(c * kc, kc), kc)
        n = t * CHUNKS + c
        pltpu.make_async_remote_copy(
            gat.at[block, :, cols], gat.at[block, :, cols], up_s.at[n], up_r.at[n],
            device_id={"blk": lax.rem(blk + 1, blocks)}, device_id_type=MESH).wait_recv()

    def dn_wait(t, c):
        block = lax.rem(blk + 1 + t, blocks)
        cols = pl.ds(pl.multiple_of(c * kc, kc), kc)
        n = t * CHUNKS + c
        pltpu.make_async_remote_copy(
            gat.at[block, :, cols], gat.at[block, :, cols], dn_s.at[n], dn_r.at[n],
            device_id={"blk": lax.rem(blk + 1, blocks)}, device_id_type=MESH).wait_recv()

    load, prepare, one_head = attention(
        (cache, qf, qs, cf, kv_sem),
        q_ref, kv_ref, draft_ref, len_ref, acc_ref, gat, blk)
    load()
    for c in range(CHUNKS):
        w_copy(c).start()

    barrier = pltpu.get_barrier_semaphore()
    for k in range(1, blocks):
        pl.semaphore_signal(barrier, inc=1, device_id={"blk": lax.rem(blk + k, blocks)},
                            device_id_type=MESH)
    pl.semaphore_signal(barrier, inc=1, device_id={"head": partner}, device_id_type=MESH)
    for k in range(1, pairs):
        pl.semaphore_signal(
            barrier, inc=1,
            device_id={"head": lax.rem(chip + k, pairs) * 2 + side}, device_id_type=MESH)
    prepare()
    one_head(0)
    pl.semaphore_wait(barrier, blocks - 1 + 1 + pairs - 1)

    inner = jnp.logical_and(blk > 0, blk + 1 < blocks)

    def send_own(c):
        @pl.when(blk + 1 < blocks)
        def _():
            up_copy(0, c).start()

        @pl.when(blk > 0)
        def _():
            dn_copy(0, c).start()

    def forward(c):
        def one(t, carry):
            @pl.when(jnp.logical_and(inner, blk - 1 - t >= 0))
            def _():
                up_wait(t, c)
                up_copy(t + 1, c).start()

            @pl.when(jnp.logical_and(inner, blk + 1 + t < blocks))
            def _():
                dn_wait(t, c)
                dn_copy(t + 1, c).start()

            return carry

        lax.fori_loop(0, blocks - 2, one, 0)

    for kh in range(kvh):
        if kh:
            one_head(kh)
        for c in range(kh * ready, (kh + 1) * ready):
            send_own(c)
    for c in range(CHUNKS):
        forward(c)

    def arrived(c):
        w_copy(c).wait()

        def one(t, carry):
            @pl.when(blk == blocks - 1)
            def _():
                up_wait(t, c)

            @pl.when(blk == 0)
            def _():
                dn_wait(t, c)

            return carry

        lax.fori_loop(0, blocks - 1, one, 0)

    def product(c, n):
        x = gat[:, :, c * kc:(c + 1) * kc].reshape(blocks * rows, kc)
        return jnp.dot(x, wv[c * kc:(c + 1) * kc, n], preferred_element_type=jnp.float32)

    def add_chunk(c):
        def tile_of(j, carry):
            n = pl.ds(pl.multiple_of(j * nt, nt), nt)
            if c == 0:
                acc[:, n] = product(c, n)
            else:
                acc[:, n] = acc[:, n] + product(c, n)
            return carry

        lax.fori_loop(0, tiles, tile_of, 0)

    for c in range(CHUNKS - 1):
        arrived(c)
        add_chunk(c)

    arrived(CHUNKS - 1)

    def a_copy(j):
        return pltpu.make_async_remote_copy(
            send_a.at[j], recv_a.at[j], a_s.at[j], a_r.at[j],
            device_id={"head": partner}, device_id_type=MESH)

    def b_copy(j, k):
        to = lax.rem(chip + k, pairs)
        n = j * (pairs - 1) + k - 1
        return pltpu.make_async_remote_copy(
            send_b.at[n], recv_b.at[n], b_s.at[n], b_r.at[n],
            device_id={"head": to * 2 + side}, device_id_type=MESH)

    def pair_sum(j):
        n = pl.ds(pl.multiple_of(j * nt, nt), nt)
        a_copy(j).wait_recv()
        for k in range(pairs):
            to = lax.rem(chip + k, pairs)
            at = pl.ds(pl.multiple_of((to * 2 + side) * own_rows, own_rows), own_rows)
            total = acc[at, n] + recv_a[j, to].astype(jnp.float32)
            if k == 0:
                acc[at, n] = total
            else:
                send_b[j * (pairs - 1) + k - 1] = total.astype(jnp.bfloat16)
                b_copy(j, k).start()

    def last(j, carry):
        n = pl.ds(pl.multiple_of(j * nt, nt), nt)
        acc[:, n] = acc[:, n] + product(CHUNKS - 1, n)
        for x in range(pairs):
            at = pl.ds(pl.multiple_of((x * 2 + 1 - side) * own_rows, own_rows), own_rows)
            send_a[j, x] = acc[at, n].astype(jnp.bfloat16)
        a_copy(j).start()

        @pl.when(j > 0)
        def _():
            pair_sum(j - 1)

        return carry

    lax.fori_loop(0, tiles, last, 0)
    pair_sum(tiles - 1)

    squares[blk] = jnp.zeros((own_rows, 128), jnp.float32)
    mine = pl.ds(pl.multiple_of(head * own_rows, own_rows), own_rows)

    def finish(j, carry):
        n = pl.ds(pl.multiple_of(j * nt, nt), nt)
        total = acc[mine, n]
        for k in range(1, pairs):
            b_copy(j, k).wait_recv()
            total = total + recv_b[j * (pairs - 1) + k - 1].astype(jnp.float32)
        total = total + res_ref[:, n].astype(jnp.float32)
        sum_ref[:, n] = total
        power = total * total
        part = power[:, 0:128]
        for v in range(1, nt // 128):
            part = part + power[:, v * 128:(v + 1) * 128]
        squares[blk] = squares[blk] + part
        return carry

    lax.fori_loop(0, tiles, finish, 0)

    def q_copy(k):
        return pltpu.make_async_remote_copy(
            squares.at[blk], squares.at[blk], q_s.at[k - 1], q_r.at[k - 1],
            device_id={"blk": lax.rem(blk + k, blocks)}, device_id_type=MESH)

    for k in range(1, blocks):
        q_copy(k).start()
    for k in range(1, blocks):
        src = lax.rem(blk - k + blocks, blocks)
        pltpu.make_async_remote_copy(
            squares.at[src], squares.at[src], q_s.at[k - 1], q_r.at[k - 1],
            device_id={"blk": lax.rem(blk + k, blocks)}, device_id_type=MESH).wait_recv()

    spread = squares[0]
    for b in range(1, blocks):
        spread = spread + squares[b]
    inverse = lax.rsqrt(jnp.sum(spread, axis=1, keepdims=True) / full + 1e-5)
    inv_ref[...] = inverse

    for c in range(CHUNKS):
        @pl.when(blk + 1 < blocks)
        def _():
            up_copy(0, c).wait_send()

        @pl.when(blk > 0)
        def _():
            dn_copy(0, c).wait_send()

    def forwarded(n, carry):
        t = n // CHUNKS
        c = lax.rem(n, CHUNKS)

        @pl.when(jnp.logical_and(inner, blk - 1 - t >= 0))
        def _():
            up_copy(t + 1, c).wait_send()

        @pl.when(jnp.logical_and(inner, blk + 1 + t < blocks))
        def _():
            dn_copy(t + 1, c).wait_send()

        return carry

    lax.fori_loop(0, (blocks - 2) * CHUNKS, forwarded, 0)

    def tile_sent(j, carry):
        a_copy(j).wait_send()
        for k in range(1, pairs):
            b_copy(j, k).wait_send()
        return carry

    lax.fori_loop(0, tiles, tile_sent, 0)
    for k in range(1, blocks):
        q_copy(k).wait_send()


def local(blocks, heads, queries, kv_cache, draft_kv, cache_len, accepted, w_out, residual,
          norm_gain):
    rows, depth = queries.shape
    seqs, slots, kvh, two = kv_cache.shape
    hd = two // 2
    drafts = draft_kv.shape[1]
    wide = w_out.shape[1]
    own_rows = residual.shape[0]
    nt = min(TILE, wide)
    tiles = wide // nt
    pairs = heads // 2
    hops = (blocks - 1) * CHUNKS
    cross = max(tiles * (pairs - 1), 1)
    dma = pltpu.SemaphoreType.DMA
    vmem = pl.BlockSpec(memory_space=pltpu.VMEM)
    smem = pl.BlockSpec(memory_space=pltpu.SMEM)
    anywhere = pl.BlockSpec(memory_space=pl.ANY)
    summed, inverse = pl.pallas_call(
        functools.partial(project_kernel, blocks, heads),
        out_shape=(
            jax.ShapeDtypeStruct((own_rows, wide), jnp.float32),
            jax.ShapeDtypeStruct((own_rows, 1), jnp.float32),
        ),
        in_specs=[vmem, anywhere, vmem, smem, smem, anywhere, vmem],
        out_specs=(vmem, vmem),
        scratch_shapes=[
            pltpu.VMEM((seqs, slots, kvh, two), jnp.bfloat16),
            pltpu.VMEM((rows, depth), jnp.float32),
            pltpu.VMEM((seqs, depth // hd * drafts, hd), jnp.float32),
            pltpu.VMEM((rows, depth), jnp.float32),
            dma((seqs,)),
            pltpu.VMEM((blocks, rows, depth), jnp.bfloat16),
            pltpu.VMEM((depth, wide), jnp.bfloat16),
            pltpu.VMEM((blocks * rows, wide), jnp.float32),
            pltpu.VMEM((tiles, pairs, own_rows, nt), jnp.bfloat16),
            pltpu.VMEM((tiles, pairs, own_rows, nt), jnp.bfloat16),
            pltpu.VMEM((cross, own_rows, nt), jnp.bfloat16),
            pltpu.VMEM((cross, own_rows, nt), jnp.bfloat16),
            pltpu.VMEM((blocks, own_rows, 128), jnp.float32),
            dma((CHUNKS,)),
            dma((hops,)), dma((hops,)), dma((hops,)), dma((hops,)),
            dma((tiles,)), dma((tiles,)),
            dma((cross,)), dma((cross,)),
            dma((blocks - 1,)), dma((blocks - 1,)),
        ],
        compiler_params=pltpu.CompilerParams(
            collective_id=0, has_side_effects=True, vmem_limit_bytes=56 * 2**20),
        cost_estimate=pl.CostEstimate(
            flops=2 * blocks * rows * depth * wide, bytes_accessed=2 * depth * wide,
            transcendentals=0),
        name="project",
    )(queries, kv_cache, draft_kv, cache_len, accepted.T, w_out, residual)
    normed = summed * inverse * norm_gain.astype(jnp.float32)[None, :]
    return (summed.astype(jnp.bfloat16), normed.astype(jnp.bfloat16))


def solution(mesh):
    return jax.shard_map(
        functools.partial(local, mesh.shape["blk"], mesh.shape["head"]),
        mesh=mesh,
        in_specs=(
            P(("grp", "blk"), "head"),
            P(("grp", "blk"), None, "head", None),
            P(("grp", "blk"), None, "head", None),
            P(("grp", "blk")),
            P(("grp", "blk"), None),
            P("head", "blk"),
            P(("grp", "head"), "blk"),
            P("blk"),
        ),
        out_specs=(P(("grp", "head"), "blk"), P(("grp", "head"), "blk")),
        check_vma=False,
    )
```
